512 devices in a mesh: dp: 64 (over z, y), section: 8 (over x, core).
Axes of the slice: x: 4, y: 4, z: 16, core: 2. Of those that a mesh axis runs over, the one named last changes fastest.
Arguments:
- section_rows: bfloat16 [8, 8192, 2048], P('section', 'dp'), may hold values from -16 to 16
- embedded: bfloat16 [8192, 2048], P('dp'), may hold values from -16 to 16
- norm_gain: float32 [8, 1024], P('section'), may hold values from 0.1 to 1.9
- routes: int32 [8, 8192, 6], P('section', 'dp'), may hold values from 0 to 63, all different within a row; in each aligned block of 128 rows (0 to 127, 128 to 255, ..., all dimensions but the last counted through in order) at most 16 rows name the same one
- out_grad: bfloat16 [8, 8192, 6, 704], P('section', 'dp'), may hold values from -6 to 6
- momentum: bfloat16 [8, 64, 1024, 704], P('section', None, 'dp'), may hold values from -120 to 120
Outputs:
- update: bfloat16 [8, 64, 1024, 704], P('section', None, 'dp')
The draws below stay inside these ranges and needn't reach their ends.
Inputs may be any that keep to these rules, and one draw needn't show every extreme that they name: `routes`: among the rows of one device no expert is named by more than 16 of its slots; some expert is named by exactly 16 in some of them.
All inputs are finite; a program needn't handle non-finite values.
Results may differ from the reference program's by a relative error of at most 0.018.
Values may be sent and summed in bfloat16 or wider, within the bound.
A program may use at most 64 MiB of HBM per device.

```python
import math
import jax
import jax.numpy as jnp
import numpy as np
from jax import lax

D = 2048
TOP = 6
DW = 1024
FW = 704
TOK_DEV = 128
NS_ITERS = 2
EXPERTS = 64
SECTIONS = 8
TOKENS = 8192
CAP = 16
N_DP = 64


def with_spikes(result, stream_key, source, target, shards_of, factor):
    def block_of(position):
        return (jnp.arange(result.shape[position]) // (result.shape[position] // shards_of)).reshape((-1,) + (1,) * (result.ndim - 1 - position))

    one_side = jax.random.permutation(stream_key, shards_of)[block_of(target)]
    second = (block_of(target) + shards_of // 2) % shards_of
    return jnp.where((block_of(source) == one_side) | (block_of(source) == second), factor * result, result)


def level_of(key, extent, shards, least, largest):
    factor_of, own = 1.0, jax.random.fold_in(key, 6)
    for position, shards_of in shards:
        steps = jnp.exp(jax.random.uniform(jax.random.fold_in(own, position), (shards_of,), jnp.float32, least / len(shards), largest / len(shards)))
        factor_of = factor_of * jnp.repeat(steps, extent[position] // shards_of).reshape([-1 if axis == position else 1 for axis in range(len(extent))])
    return factor_of


def deal_out(own_key, own, number, rows, amount, top, most, slope):
    sequence = jax.random.permutation(own_key, amount)
    crowded, ordinary = shares(amount, rows * top, most, slope, True), shares(amount, rows * top, most, slope, False)
    places = jnp.arange(amount)

    def named(sizes, rotation):
        used = int((sizes > 0).sum())
        fixed = max(1, used // 4)
        shifted = fixed + (places - fixed + rotation * (used - fixed)) % max(1, amount - fixed)
        return jnp.zeros((amount,), jnp.int32).at[sequence[jnp.where(places < fixed, places, shifted)]].set(jnp.asarray(sizes, jnp.int32))

    sizes = jnp.where(number % 4 == 0, named(crowded, number // 4), named(ordinary, number - number // 4 - 1))
    mixed = jax.random.permutation(jax.random.fold_in(own, 3), amount)
    giver, receiver = mixed[0:amount // 2 * 2:2], mixed[1:amount // 2 * 2:2]
    room = jnp.minimum(sizes[giver] - 1, most - sizes[receiver]) // 2
    room = jnp.where((giver == sequence[0]) | (receiver == sequence[0]) | (sizes[receiver] == 0), 0, jnp.maximum(room, 0))
    shifted = jax.random.randint(jax.random.fold_in(own, 4), (amount // 2,), 0, 1 << 20) % (room + 1)
    sizes = sizes.at[giver].add(-shifted).at[receiver].add(shifted)
    members = jnp.searchsorted(jnp.cumsum(sizes), jnp.arange(rows * top), side="right").astype(jnp.int32)
    listing = members.reshape(top, rows).T
    listing = listing[jax.random.permutation(jax.random.fold_in(own, 1), rows)]
    rotation = jax.random.randint(jax.random.fold_in(own, 2), (rows, 1), 0, top)
    return jnp.take_along_axis(listing, (jnp.arange(top)[None, :] + rotation) % top, axis=1)


def shares(number_of, total, reach, lean, full):
    loads = [(1 << 20) // math.isqrt(standing ** lean) + 1 for standing in range(1, number_of + 1)]
    largest = reach if full else min(reach, max(-(-total // number_of), total * loads[0] // sum(loads)))
    least = 1 if total - largest >= number_of - 1 else 0
    holding, rest = [largest] + [least] * (number_of - 1), total - largest - least * (number_of - 1)
    while rest > 0:
        movable = [i for i in range(1, number_of) if holding[i] < largest] or [i for i in range(1, number_of) if holding[i] < reach]
        mass, budget = sum([loads[i] for i in movable]), rest
        for i in movable:
            addition = min(reach - holding[i], max(1, budget * loads[i] // mass), rest)
            holding[i] = holding[i] + addition
            rest = rest - addition
    return np.array(holding)


def bell_draw(rng, shape, scale, reach, cuts=(), held_as=jnp.bfloat16):
    result = jax.random.normal(rng, shape, jnp.float32) * scale
    if len(cuts) > 0:
        result = level_of(rng, shape, cuts, -0.22, 0.18) * result
    return jnp.clip(result, min=-reach, max=reach).astype(held_as)


def bell_draw_with(own_key, extent, spread, most, split, heavy, kind=jnp.bfloat16):
    array = spread * jax.random.normal(own_key, extent, jnp.float32)
    if split:
        array = array * level_of(own_key, extent, split, -0.22, 0.18)
    return jnp.clip(with_spikes(array, jax.random.fold_in(own_key, 3), *heavy), -most, most).astype(kind)


def setup_inputs(seed: int = 0) -> dict:
    keys = jax.random.split(jax.random.key(seed), 7)
    section_rows = bell_draw_with(keys[0], (SECTIONS, TOKENS, D), 1.0, 16.0, ((0, 8), (1, 64)), (1, 2, 64, 4.0))
    embedded = bell_draw_with(keys[1], (TOKENS, D), 1.0, 16.0, ((0, 64),), (0, 1, 64, 4.0))
    norm_gain = jnp.clip(1.0 + 0.18 * jax.random.normal(keys[2], (SECTIONS, DW), jnp.float32), 0.1, 1.9)
    routes_keys = jax.random.split(jax.random.fold_in(keys[3], 1), SECTIONS * TOKENS // TOK_DEV)
    routes_turns = jax.random.permutation(jax.random.fold_in(keys[3], 3), SECTIONS * TOKENS // TOK_DEV)
    routes = jax.vmap(lambda own, number: deal_out(jax.random.fold_in(keys[3], 2), own, number, TOK_DEV, EXPERTS, TOP, CAP, 1))(routes_keys, routes_turns).reshape((SECTIONS, TOKENS, TOP))
    out_grad = bell_draw(keys[4], (SECTIONS, TOKENS, TOP, FW), 1.0, 6.0, ((0, 8), (1, 64)))
    momentum = bell_draw(keys[5], (SECTIONS, EXPERTS, DW, FW), 20.0, 120.0, ((0, 8), (2, 64)))
    return {"section_rows": section_rows, "embedded": embedded, "norm_gain": norm_gain, "routes": routes, "out_grad": out_grad, "momentum": momentum}


COEF_A = 3.4445
COEF_B = -4.775
COEF_C = 2.0315
MOMENTUM_RATE = 0.95
NORM_EPS = 1e-06

def window_features(rows, gain_row):
    values = rows.astype(jnp.float32)
    inverse = lax.rsqrt(lax.optimization_barrier(jnp.mean(values * values, axis=-1, keepdims=True)) + NORM_EPS)
    width = gain_row.shape[-1]
    return (values[:, :width] * inverse * gain_row).astype(jnp.bfloat16)

def newton_schulz(gradient, momentum_rows):
    blended = gradient + MOMENTUM_RATE * (MOMENTUM_RATE * momentum_rows.astype(jnp.float32) + gradient)
    frobenius = jnp.sqrt(jnp.sum(blended * blended))
    iterate = (blended / (frobenius + 1e-07)).astype(jnp.bfloat16)
    for repeat in range(NS_ITERS):
        gram = lax.dot_general(iterate, iterate, (((0,), (0,)), ((), ())), preferred_element_type=jnp.float32).astype(jnp.bfloat16)
        squared = jnp.dot(gram, gram, preferred_element_type=jnp.float32)
        polynomial = (COEF_B * gram.astype(jnp.float32) + COEF_C * squared).astype(jnp.bfloat16)
        iterate = (COEF_A * iterate.astype(jnp.float32) + jnp.dot(iterate, polynomial, preferred_element_type=jnp.float32)).astype(jnp.bfloat16)
    factor = 0.2 * math.sqrt(iterate.shape[0])
    return (factor * iterate.astype(jnp.float32)).astype(jnp.bfloat16)

def reference(section_rows, embedded, norm_gain, routes, out_grad, momentum):
    inputs = jnp.concatenate([embedded[None], section_rows[:-1]], axis=0)
    limit = N_DP * CAP
    slots = TOKENS * TOP

    def one_section(packed):
        rows, gain_row, route_block, grad_block, moment_block = packed
        features = window_features(rows, gain_row)
        flat = route_block.reshape(-1).astype(jnp.int32)
        order = jnp.argsort(flat, stable=True).astype(jnp.int32)
        counts = lax.optimization_barrier(jnp.sum((flat[:, None] == jnp.arange(EXPERTS, dtype=jnp.int32)[None, :]).astype(jnp.int32), axis=0)).astype(jnp.int32)
        starts = (jnp.cumsum(counts) - counts).astype(jnp.int32)
        token_of = jnp.concatenate([(order // TOP).astype(jnp.int32), jnp.zeros((limit,), jnp.int32)])
        grad_rows = jnp.concatenate([grad_block.reshape(slots, FW)[order], jnp.zeros((limit, FW), jnp.bfloat16)], axis=0)

        def one_expert(packed_expert):
            start, count, moment_rows = packed_expert
            picked = lax.dynamic_slice(token_of, (start.astype(jnp.int32),), (limit,))
            live = jnp.arange(limit, dtype=jnp.int32) < count
            left = features[picked]
            chosen = lax.dynamic_slice(grad_rows, (start.astype(jnp.int32), jnp.int32(0)), (limit, FW))
            right = jnp.where(live[:, None], chosen, jnp.zeros((), jnp.bfloat16))
            gradient = lax.dot_general(left, right, (((0,), (0,)), ((), ())), preferred_element_type=jnp.float32)
            return newton_schulz(gradient, moment_rows)
        return lax.map(one_expert, (starts, counts, moment_block))
    return lax.map(one_section, (inputs, norm_gain, routes, out_grad, momentum))
```

```python
import functools
import math

import jax
import jax.numpy as jnp
from jax import lax
from jax.experimental import pallas as pl
from jax.experimental.pallas import tpu as pltpu
from jax.sharding import PartitionSpec as P

MESH = pl.DeviceIdType.MESH
F32 = jnp.float32
BF16 = jnp.bfloat16

NS_ITERS = 2
COEF_A = 3.4445
COEF_B = -4.775
COEF_C = 2.0315
MOMENTUM_RATE = 0.95
NORM_EPS = 1e-06

NY = 4
CAP = 16
PAD = 8
LANES = 128


def iota(shape, dim):
    return lax.broadcasted_iota(jnp.int32, shape, dim)


def kernel(
    n_dp,
    n_sec,
    rows_ref,
    emb_ref,
    gain_ref,
    routes_ref,
    gt_ref,
    mom_ref,
    out_ref,
    rrecv,
    fall,
    wk,
    pmsend,
    pmrecv,
    gsc,
    gsend,
    mrecv,
    grecv,
    ysend,
    frecv,
    bl,
    xs,
    gram,
    poly,
    upd,
    x_sem,
    m_sem,
    g_sem,
    p_sem,
    y_sem,
    u_sem,
    ring_send,
    ring_recv,
):
    nz = n_dp // NY
    half = nz // 2
    top, hidden, tokens = gt_ref.shape
    width = gain_ref.shape[1]
    block = mom_ref.shape[1]
    main = mrecv.shape[1]
    padded = grecv.shape[1]
    tail = hidden - main
    group = NY * CAP

    me = lax.axis_index("dp")
    sec = lax.axis_index("section")
    z = me // NY
    y = me % NY

    def wrap(index):
        return lax.rem(index + nz, nz)

    def remote(src, dst, sems, to_z, to_y):
        return pltpu.make_async_remote_copy(
            src_ref=src,
            dst_ref=dst,
            send_sem=sems.at[0],
            recv_sem=sems.at[1],
            device_id=(to_z * NY + to_y, sec),
            device_id_type=MESH,
        )

    def take(ref, sem):
        pltpu.make_async_copy(ref, ref, sem).wait()

    def rows_at(ref, start, size):
        return ref.at[pl.ds(pl.multiple_of(start, size), size)]

    barrier = pltpu.get_barrier_semaphore()
    after = lax.rem(sec + 1, n_sec)
    before = lax.rem(sec + n_sec - 1, n_sec)

    def greet(k, carry):
        pl.semaphore_signal(
            barrier, inc=1, device_id=(lax.rem(me + k, n_dp), sec), device_id_type=MESH
        )
        return carry

    lax.fori_loop(1, n_dp, greet, 0)
    for other in (after, before):
        pl.semaphore_signal(barrier, inc=1, device_id=(me, other), device_id_type=MESH)
    pl.semaphore_wait(barrier, n_dp + 1)

    section_copy = pltpu.make_async_remote_copy(
        src_ref=rows_ref,
        dst_ref=rrecv,
        send_sem=x_sem.at[0],
        recv_sem=x_sem.at[1],
        device_id=(me, after),
        device_id_type=MESH,
    )
    section_copy.start()

    same_parity = lax.rem(z, 2)

    def offset(phase, jz):
        near = half - 2 * ((jz + 1) // 2)
        near = jnp.where(jz % 2 == 1, near, -near)
        odd = half - 1 - 2 * (jz // 2)
        odd = jnp.where(jz % 2 == 0, odd, -odd)
        return jnp.where(same_parity == phase, near, odd)

    def send_to(src, dst, sems, to_z, to_y):
        target = to_z * NY + to_y

        @pl.when(target != me)
        def _():
            remote(src, dst, sems, to_z, to_y).start()

        @pl.when(target == me)
        def _():
            pltpu.make_async_copy(src, dst, sems.at[1]).start()

    def send_momentum(phase, lo, hi):
        def one(j, carry):
            to_z = wrap(z + offset(phase, j // NY))
            to_y = lax.rem(y + j % NY, NY)
            send_to(
                mom_ref.at[to_z * NY + to_y, :, pl.ds(0, main)],
                rows_at(mrecv, block * me, block),
                m_sem,
                to_z,
                to_y,
            )
            return carry

        lax.fori_loop(lo, hi, one, 0)

    send_momentum(0, 0, half * NY)

    table = nz * PAD
    expert = iota((table, tokens), 0)
    expert = jnp.where(expert % PAD < NY, (expert // PAD) * NY + expert % PAD, -1)
    named = jnp.zeros((table, tokens), F32)
    for k in range(top):
        named += jnp.where(routes_ref[k : k + 1, :] == expert, 1.0, 0.0)
    earlier = jnp.where(iota((tokens, tokens), 0) < iota((tokens, tokens), 1), 1.0, 0.0)
    place = jnp.dot(named.astype(BF16), earlier.astype(BF16), preferred_element_type=F32)
    for k in range(top):
        wk[k] = jnp.where(routes_ref[k : k + 1, :] == expert, place, -1.0).astype(BF16)
    pmsend[...] = jnp.where(named > 0.0, place, -1.0)

    def send_places(dz, carry):
        to_z = wrap(z + dz)
        send_to(rows_at(pmsend, PAD * to_z, PAD), rows_at(pmrecv, PAD * z, PAD), p_sem, to_z, y)
        return carry

    lax.fori_loop(0, nz, send_places, 0)

    for k in range(top):
        widened = jnp.concatenate(
            [gt_ref[k], jnp.zeros((padded - hidden, tokens), BF16)], axis=0
        )
        gsc[k * tokens : (k + 1) * tokens, :] = widened.T

    section_copy.wait_recv()
    values = jnp.where(sec == 0, emb_ref[...], rrecv[...]).astype(F32)
    inverse = lax.rsqrt(jnp.mean(values * values, axis=-1, keepdims=True) + NORM_EPS)
    fall[pl.ds(pl.multiple_of(z * tokens, tokens), tokens), :] = (
        values[:, :width] * inverse * gain_ref[...]
    ).astype(BF16)

    directions = ((0, 1, half), (1, -1, half - 1))

    def ring_copy(di, d, step):
        part = rows_at(fall, wrap(z - d * step) * tokens, tokens)
        return pltpu.make_async_remote_copy(
            src_ref=part,
            dst_ref=part,
            send_sem=ring_send.at[di, step],
            recv_sem=ring_recv.at[di, step],
            device_id=(wrap(z + d) * NY + y, sec),
            device_id_type=MESH,
        )

    def ring_step(step):
        for di, d, count in directions:
            if 1 <= step <= count:
                ring_copy(di, d, step - 1).wait_recv()
            if step < count:
                ring_copy(di, d, step).start()

    slots = 4 * group
    shift = jnp.where(
        iota((tail, LANES), 1) == iota((tail, LANES), 0) + (LANES - tail), 1.0, 0.0
    ).astype(BF16)
    chunks = half // 4

    def pack(phase, q):
        base = (phase * chunks + q) * slots
        to = [wrap(z + offset(phase, 4 * q + i)) for i in range(4)]
        which = iota((slots, table), 0)
        row = jnp.zeros((slots, table), jnp.int32)
        for i in range(4):
            row = jnp.where(which // group == i, to[i] * PAD, row)
        row = row + (which // CAP) % NY
        spread = jnp.where(iota((slots, table), 1) == row, 1.0, 0.0).astype(BF16)
        spot = (iota((slots, tokens), 0) % CAP).astype(F32)
        picks = []
        for k in range(top):
            at = jnp.dot(spread, wk[k], preferred_element_type=F32)
            picks.append(jnp.where(at == spot, 1.0, 0.0).astype(BF16))
        chosen = jnp.dot(jnp.concatenate(picks, axis=1), gsc[...], preferred_element_type=F32)
        gsend[base : base + slots, :main] = chosen[:, :main].astype(BF16)
        tails = jnp.concatenate(
            [
                mom_ref[pl.ds(to[i] * NY, NY), :, main:hidden].reshape(NY * block, tail)
                for i in range(4)
            ],
            axis=0,
        )
        gsend[base : base + slots, main:] = (
            chosen[:, main:] + jnp.dot(tails, shift, preferred_element_type=F32)
        ).astype(BF16)

        def one(j, carry):
            to_z = wrap(z + offset(phase, 4 * q + j // NY))
            to_y = j % NY
            send_to(
                rows_at(gsend, base + j * CAP, CAP),
                rows_at(grecv, CAP * me, CAP),
                g_sem,
                to_z,
                to_y,
            )
            return carry

        lax.fori_loop(0, 4 * NY, one, 0)

    def pick(source):
        places = pmrecv[pl.ds(pl.multiple_of(source * PAD, PAD), PAD), :]
        at = jnp.concatenate(
            [jnp.broadcast_to(places[i : i + 1, :], (CAP, tokens)) for i in range(NY)], axis=0
        )
        spot = (iota((group, tokens), 0) % CAP).astype(F32)
        chosen = jnp.dot(
            jnp.where(at == spot, 1.0, 0.0).astype(BF16),
            fall[pl.ds(pl.multiple_of(source * tokens, tokens), tokens), :],
            preferred_element_type=F32,
        )
        ysend[pl.ds(pl.multiple_of(source * group, group), group), :] = chosen.astype(BF16)
        for dy in range(NY):
            to_y = lax.rem(y + dy, NY)
            src = rows_at(ysend, source * group + to_y * CAP, CAP)
            dst = rows_at(frecv, (source * NY + y) * CAP, CAP)
            if dy == 0:
                pltpu.make_async_copy(src, dst, y_sem.at[1]).start()
            else:
                remote(src, dst, y_sem, z, to_y).start()

    def pick_step(step):
        pick(wrap(z + step))
        if 0 < step < half:
            pick(wrap(z - step))

    fillers = [functools.partial(pack, 0, q) for q in range(chunks)]
    fillers.append(functools.partial(send_momentum, 1, 0, half * NY))
    fillers += [functools.partial(pack, 1, q) for q in range(chunks)]
    slots_for = {1: 0, 3: 1, 5: 2, 6: 3, 7: 4}
    for step in range(half + 1):
        ring_step(step)
        if step == 0:
            take(pmrecv, p_sem.at[1])
        pick_step(step)
        for at_step, index in slots_for.items():
            if min(at_step, half) == step and index < len(fillers):
                fillers[index]()

    take(frecv, y_sem.at[1])
    take(grecv, g_sem.at[1])
    take(mrecv, m_sem.at[1])
    tile = 256
    tiles = width // tile

    def blend(t, total):
        rows = pl.ds(pl.multiple_of(t * tile, tile), tile)
        cols = pl.ds(pl.multiple_of(t * tile, tile), tile)
        gradient = lax.dot_general(
            frecv[:, cols], grecv[...], (((0,), (0,)), ((), ())), preferred_element_type=F32
        )

        def mixed(grad, mom):
            return grad + MOMENTUM_RATE * (MOMENTUM_RATE * mom + grad)

        first = mixed(gradient[:, :main], mrecv[rows, :].astype(F32))
        rest = pltpu.roll(grecv[rows, main:].astype(F32), tail, 1)
        last = mixed(gradient[:, main:], rest)
        last = jnp.where(iota(last.shape, 1) < tail, last, 0.0)
        bl[rows, :main] = first
        bl[rows, main:] = last
        return total + jnp.sum(first * first) + jnp.sum(last * last)

    total = lax.fori_loop(0, tiles, blend, jnp.zeros((), F32))
    scale = 1.0 / (jnp.sqrt(jnp.full((1, 1), total, F32)) + 1e-07)

    def normalize(t, carry):
        rows = pl.ds(pl.multiple_of(t * tile, tile), tile)
        xs[rows, :] = (bl[rows, :] * scale).astype(BF16)
        return carry

    lax.fori_loop(0, tiles, normalize, 0)

    factor = 0.2 * math.sqrt(width)
    for repeat in range(NS_ITERS):
        last_one = repeat == NS_ITERS - 1

        def make_gram(t, carry):
            cols = pl.ds(pl.multiple_of(t * tile, tile), tile)
            gram[cols, :] = lax.dot_general(
                xs[:, cols], xs[...], (((0,), (0,)), ((), ())), preferred_element_type=F32
            ).astype(BF16)
            return carry

        def make_poly(t, carry):
            rows = pl.ds(pl.multiple_of(t * tile, tile), tile)
            here = gram[rows, :]
            squared = jnp.dot(here, gram[...], preferred_element_type=F32)
            poly[rows, :] = (COEF_B * here.astype(F32) + COEF_C * squared).astype(BF16)
            return carry

        def make_iterate(k, carry):
            t = lax.rem(z // (tile // (NY * block)) + k, tiles)
            rows = pl.ds(pl.multiple_of(t * tile, tile), tile)
            here = xs[rows, :]
            fresh = (
                COEF_A * here.astype(F32) + jnp.dot(here, poly[...], preferred_element_type=F32)
            ).astype(BF16)
            if not last_one:
                xs[rows, :] = fresh
                return carry
            upd[rows, :] = (factor * fresh.astype(F32)).astype(BF16)[:, :hidden]

            def one(j, inner):
                target = t * (tile // block) + j
                send_to(
                    rows_at(upd, target * block, block),
                    out_ref.at[me],
                    u_sem,
                    target // NY,
                    target % NY,
                )
                return inner

            lax.fori_loop(0, tile // block, one, 0)
            return carry

        lax.fori_loop(0, padded // tile, make_gram, 0)
        lax.fori_loop(0, padded // tile, make_poly, 0)
        lax.fori_loop(0, tiles, make_iterate, 0)

    section_copy.wait_send()
    others = n_dp - 1
    take(mrecv.at[pl.ds(0, others * block)], m_sem.at[0])
    take(grecv.at[pl.ds(0, others * CAP)], g_sem.at[0])
    take(pmsend.at[pl.ds(0, (nz - 1) * PAD)], p_sem.at[0])
    take(frecv.at[pl.ds(0, nz * (NY - 1) * CAP)], y_sem.at[0])
    for di, d, count in directions:
        for step in range(count):
            ring_copy(di, d, step).wait_send()
    take(upd.at[pl.ds(0, others * block)], u_sem.at[0])
    take(out_ref, u_sem.at[1])


def on_device(section_rows, embedded, norm_gain, routes, out_grad, momentum):
    n_dp = lax.axis_size("dp")
    n_sec = lax.axis_size("section")
    nz = n_dp // NY
    half = nz // 2
    tokens, top, hidden = out_grad.shape[1:]
    experts, block = momentum.shape[1:3]
    width = norm_gain.shape[1]
    padded = -(-hidden // 256) * 256
    main = hidden // LANES * LANES
    slots = n_dp * CAP
    vmem = pl.BlockSpec(memory_space=pltpu.VMEM)
    pair = pltpu.SemaphoreType.DMA((2,))
    return pl.pallas_call(
        functools.partial(kernel, n_dp, n_sec),
        out_shape=jax.ShapeDtypeStruct((experts, block, hidden), BF16),
        in_specs=[vmem] * 6,
        out_specs=vmem,
        scratch_shapes=[
            pltpu.VMEM(section_rows.shape[1:], BF16),
            pltpu.VMEM((nz * tokens, width), BF16),
            pltpu.VMEM((top, nz * PAD, tokens), BF16),
            pltpu.VMEM((nz * PAD, tokens), F32),
            pltpu.VMEM((nz * PAD, tokens), F32),
            pltpu.VMEM((top * tokens, padded), BF16),
            pltpu.VMEM((slots, padded), BF16),
            pltpu.VMEM((n_dp * block, main), BF16),
            pltpu.VMEM((slots, padded), BF16),
            pltpu.VMEM((slots, width), BF16),
            pltpu.VMEM((slots, width), BF16),
            pltpu.VMEM((width, padded), F32),
            pltpu.VMEM((width, padded), BF16),
            pltpu.VMEM((padded, padded), BF16),
            pltpu.VMEM((padded, padded), BF16),
            pltpu.VMEM((width, hidden), BF16),
            pair,
            pair,
            pair,
            pair,
            pair,
            pair,
            pltpu.SemaphoreType.DMA((2, half)),
            pltpu.SemaphoreType.DMA((2, half)),
        ],
        compiler_params=pltpu.CompilerParams(
            collective_id=0, has_side_effects=True, vmem_limit_bytes=56 * 1024 * 1024
        ),
        name="muon_update",
    )(
        section_rows[0],
        embedded,
        norm_gain,
        routes[0].T,
        jnp.transpose(out_grad[0], (1, 2, 0)),
        momentum[0],
    )[None]


def solution(mesh):
    in_specs = (
        P("section", "dp", None),
        P("dp", None),
        P("section", None),
        P("section", "dp", None),
        P("section", "dp", None, None),
        P("section", None, "dp", None),
    )
    out_specs = P("section", None, "dp", None)
    return jax.shard_map(
        on_device, mesh=mesh, in_specs=in_specs, out_specs=out_specs, check_vma=False
    )
```

```python
import functools
import math

import jax
import jax.numpy as jnp
from jax import lax
from jax.experimental import pallas as pl
from jax.experimental.pallas import tpu as pltpu
from jax.sharding import PartitionSpec as P

MESH = pl.DeviceIdType.MESH
F32 = jnp.float32
BF16 = jnp.bfloat16

NS_ITERS = 2
COEF_A = 3.4445
COEF_B = -4.775
COEF_C = 2.0315
MOMENTUM_RATE = 0.95
NORM_EPS = 1e-06

NY = 4
CAP = 16
PAD = 8
LANES = 128

SCHEDULE = (32, 64, 64, 64, 64, 64, 64, 80, 96, 112, 128)


def iota(shape, dim):
    return lax.broadcasted_iota(jnp.int32, shape, dim)


def kernel(
    n_dp,
    n_sec,
    rows_ref,
    emb_ref,
    gain_ref,
    routes_ref,
    gt_ref,
    mom_ref,
    out_ref,
    rrecv,
    fall,
    wk,
    pmsend,
    pmrecv,
    gsc,
    gsend,
    mrecv,
    grecv,
    ysend,
    frecv,
    bl,
    xs,
    gram,
    poly,
    upd,
    tails_out,
    tails_in,
    x_sem,
    m_sem,
    g_sem,
    p_sem,
    y_sem,
    u_sem,
    t_sem,
    ring_send,
    ring_recv,
):
    nz = n_dp // NY
    half = nz // 2
    top, hidden, tokens = gt_ref.shape
    width = gain_ref.shape[1]
    block = mom_ref.shape[1]
    main = mrecv.shape[1]
    padded = grecv.shape[1]
    tail = hidden - main
    group = NY * CAP

    me = lax.axis_index("dp")
    sec = lax.axis_index("section")
    z = me // NY
    y = me % NY

    def wrap(index):
        return lax.rem(index + nz, nz)

    def remote(src, dst, sems, to_z, to_y):
        return pltpu.make_async_remote_copy(
            src_ref=src,
            dst_ref=dst,
            send_sem=sems.at[0],
            recv_sem=sems.at[1],
            device_id=(to_z * NY + to_y, sec),
            device_id_type=MESH,
        )

    def take(ref, sem):
        pltpu.make_async_copy(ref, ref, sem).wait()

    def rows_at(ref, start, size):
        return ref.at[pl.ds(pl.multiple_of(start, size), size)]

    barrier = pltpu.get_barrier_semaphore()
    after = lax.rem(sec + 1, n_sec)
    before = lax.rem(sec + n_sec - 1, n_sec)

    def greet(k, carry):
        step = (k + 1) // 2
        to = me + n_dp // 2 + jnp.where(k % 2 == 1, step, n_dp - step)
        pl.semaphore_signal(
            barrier, inc=1, device_id=(lax.rem(to, n_dp), sec), device_id_type=MESH
        )
        return carry

    lax.fori_loop(0, n_dp - 1, greet, 0)
    for other in (after, before):
        pl.semaphore_signal(barrier, inc=1, device_id=(me, other), device_id_type=MESH)
    pl.semaphore_wait(barrier, n_dp + 1)

    section_copy = pltpu.make_async_remote_copy(
        src_ref=rows_ref,
        dst_ref=rrecv,
        send_sem=x_sem.at[0],
        recv_sem=x_sem.at[1],
        device_id=(me, after),
        device_id_type=MESH,
    )
    section_copy.start()

    same_parity = lax.rem(z, 2)

    def offset(phase, jz):
        near = half - 2 * ((jz + 1) // 2)
        near = jnp.where(jz % 2 == 1, near, -near)
        odd = half - 1 - 2 * (jz // 2)
        odd = jnp.where(jz % 2 == 0, odd, -odd)
        return jnp.where(same_parity == phase, near, odd)

    def send_to(src, dst, sems, to_z, to_y):
        target = to_z * NY + to_y

        @pl.when(target != me)
        def _():
            remote(src, dst, sems, to_z, to_y).start()

        @pl.when(target == me)
        def _():
            pltpu.make_async_copy(src, dst, sems.at[1]).start()

    share = half * NY

    def stream(lo, hi):
        for part in range(4):
            first, last = max(lo, part * share), min(hi, (part + 1) * share)
            if first < last:
                lax.fori_loop(
                    first - part * share,
                    last - part * share,
                    functools.partial(send_block, part // 2, part % 2 == 1),
                    0,
                )

    def send_block(phase, cotangents, j, carry):
        to_z = wrap(z + offset(phase, j // NY))
        if cotangents:
            to_y = j % NY
            src = rows_at(gsend, (phase * share + j) * CAP, CAP)
            send_to(src, rows_at(grecv, CAP * me, CAP), g_sem, to_z, to_y)
        else:
            to_y = lax.rem(y + j, NY)
            src = mom_ref.at[to_z * NY + to_y, :, pl.ds(0, main)]
            send_to(src, rows_at(mrecv, block * me, block), m_sem, to_z, to_y)
        return carry

    stream(0, SCHEDULE[0])

    table = nz * PAD
    expert = iota((table, tokens), 0)
    expert = jnp.where(expert % PAD < NY, (expert // PAD) * NY + expert % PAD, -1)
    named = jnp.zeros((table, tokens), F32)
    for k in range(top):
        named += jnp.where(routes_ref[k] == expert, 1.0, 0.0)
    earlier = jnp.where(iota((tokens, tokens), 0) < iota((tokens, tokens), 1), 1.0, 0.0)
    place = jnp.dot(named.astype(BF16), earlier.astype(BF16), preferred_element_type=F32)
    for k in range(top):
        wk[k] = jnp.where(routes_ref[k] == expert, place, -1.0).astype(BF16)
    pmsend[...] = jnp.where(named > 0.0, place, -1.0)

    def send_places(dz, carry):
        to_z = wrap(z + dz)
        send_to(rows_at(pmsend, PAD * to_z, PAD), rows_at(pmrecv, PAD * z, PAD), p_sem, to_z, y)
        return carry

    lax.fori_loop(0, nz, send_places, 0)

    for k in range(top):
        widened = jnp.concatenate(
            [gt_ref[k], jnp.zeros((padded - hidden, tokens), BF16)], axis=0
        )
        gsc[k * tokens : (k + 1) * tokens, :] = widened.T

    slots = 4 * group
    shift = jnp.where(
        iota((tail, LANES), 1) == iota((tail, LANES), 0) + (LANES - tail), 1.0, 0.0
    ).astype(BF16)
    chunks = half // 4

    def pack(phase, q):
        base = (phase * chunks + q) * slots
        to = [wrap(z + offset(phase, 4 * q + i)) for i in range(4)]
        which = iota((slots, table), 0)
        row = jnp.zeros((slots, table), jnp.int32)
        for i in range(4):
            row = jnp.where(which // group == i, to[i] * PAD, row)
        row = row + (which // CAP) % NY
        spread = jnp.where(iota((slots, table), 1) == row, 1.0, 0.0).astype(BF16)
        spot = (iota((slots, tokens), 0) % CAP).astype(F32)
        picks = []
        for k in range(top):
            at = jnp.dot(spread, wk[k], preferred_element_type=F32)
            picks.append(jnp.where(at == spot, 1.0, 0.0).astype(BF16))
        chosen = jnp.dot(jnp.concatenate(picks, axis=1), gsc[...], preferred_element_type=F32)
        gsend[base : base + slots, :main] = chosen[:, :main].astype(BF16)
        tails = jnp.concatenate(
            [
                mom_ref[pl.ds(to[i] * NY, NY), :, main:hidden].reshape(NY * block, tail)
                for i in range(4)
            ],
            axis=0,
        )
        gsend[base : base + slots, main:] = (
            chosen[:, main:] + jnp.dot(tails, shift, preferred_element_type=F32)
        ).astype(BF16)

    for phase in range(2):
        for q in range(chunks):
            pack(phase, q)
    stream(SCHEDULE[0], SCHEDULE[1])

    section_copy.wait_recv()
    values = jnp.where(sec == 0, emb_ref[...], rrecv[...]).astype(F32)
    inverse = lax.rsqrt(jnp.mean(values * values, axis=-1, keepdims=True) + NORM_EPS)
    fall[pl.ds(pl.multiple_of(z * tokens, tokens), tokens), :] = (
        values[:, :width] * inverse * gain_ref[...]
    ).astype(BF16)

    parts = 2
    piece = tokens // parts
    ways = tuple(
        (part, way, sign, half - (part + way) % 2)
        for part in range(parts)
        for way, sign in ((0, 1), (1, -1))
    )

    def ring_copy(part, way, sign, step):
        held = rows_at(fall, wrap(z - sign * step) * tokens + part * piece, piece)
        return pltpu.make_async_remote_copy(
            src_ref=held,
            dst_ref=held,
            send_sem=ring_send.at[2 * part + way, step],
            recv_sem=ring_recv.at[2 * part + way, step],
            device_id=(wrap(z + sign) * NY + y, sec),
            device_id_type=MESH,
        )

    def ring_step(step):
        for part, way, sign, count in ways:
            if 1 <= step <= count:
                ring_copy(part, way, sign, step - 1).wait_recv()
            if step < count:
                ring_copy(part, way, sign, step).start()

    def pick(source):
        places = pmrecv[pl.ds(pl.multiple_of(source * PAD, PAD), PAD), :]
        at = jnp.concatenate(
            [jnp.broadcast_to(places[i : i + 1, :], (CAP, tokens)) for i in range(NY)], axis=0
        )
        spot = (iota((group, tokens), 0) % CAP).astype(F32)
        chosen = jnp.dot(
            jnp.where(at == spot, 1.0, 0.0).astype(BF16),
            fall[pl.ds(pl.multiple_of(source * tokens, tokens), tokens), :],
            preferred_element_type=F32,
        )
        ysend[pl.ds(pl.multiple_of(source * group, group), group), :] = chosen.astype(BF16)
        for dy in range(NY):
            to_y = lax.rem(y + dy, NY)
            src = rows_at(ysend, source * group + to_y * CAP, CAP)
            dst = rows_at(frecv, (source * NY + y) * CAP, CAP)
            if dy == 0:
                pltpu.make_async_copy(src, dst, y_sem.at[1]).start()
            else:
                remote(src, dst, y_sem, z, to_y).start()

    def pick_step(step):
        pick(wrap(z + step))
        if 0 < step < half:
            pick(wrap(z - step))

    for step in range(half + 1):
        ring_step(step)
        if step == 0:
            take(pmrecv, p_sem.at[1])
        pick_step(step)
        stream(SCHEDULE[step + 1], SCHEDULE[step + 2])

    take(frecv, y_sem.at[1])
    take(grecv, g_sem.at[1])
    take(mrecv, m_sem.at[1])
    tile = 256
    tiles = width // tile

    def blend(t, total):
        rows = pl.ds(pl.multiple_of(t * tile, tile), tile)
        cols = pl.ds(pl.multiple_of(t * tile, tile), tile)
        gradient = lax.dot_general(
            frecv[:, cols], grecv[...], (((0,), (0,)), ((), ())), preferred_element_type=F32
        )

        def mixed(grad, mom):
            return grad + MOMENTUM_RATE * (MOMENTUM_RATE * mom + grad)

        first = mixed(gradient[:, :main], mrecv[rows, :].astype(F32))
        rest = pltpu.roll(grecv[rows, main:].astype(F32), tail, 1)
        last = mixed(gradient[:, main:], rest)
        last = jnp.where(iota(last.shape, 1) < tail, last, 0.0)
        bl[rows, :main] = first
        bl[rows, main:] = last
        return total + jnp.sum(first * first) + jnp.sum(last * last)

    total = lax.fori_loop(0, tiles, blend, jnp.zeros((), F32))
    scale = 1.0 / (jnp.sqrt(jnp.full((1, 1), total, F32)) + 1e-07)

    def normalize(t, carry):
        rows = pl.ds(pl.multiple_of(t * tile, tile), tile)
        xs[rows, :] = (bl[rows, :] * scale).astype(BF16)
        return carry

    lax.fori_loop(0, tiles, normalize, 0)

    factor = 0.2 * math.sqrt(width)
    for repeat in range(NS_ITERS):
        last_one = repeat == NS_ITERS - 1

        def make_gram(t, carry):
            cols = pl.ds(pl.multiple_of(t * tile, tile), tile)
            gram[cols, :] = lax.dot_general(
                xs[:, cols], xs[...], (((0,), (0,)), ((), ())), preferred_element_type=F32
            ).astype(BF16)
            return carry

        def make_poly(t, carry):
            rows = pl.ds(pl.multiple_of(t * tile, tile), tile)
            here = gram[rows, :]
            squared = jnp.dot(here, gram[...], preferred_element_type=F32)
            poly[rows, :] = (COEF_B * here.astype(F32) + COEF_C * squared).astype(BF16)
            return carry

        def make_iterate(k, carry):
            t = lax.rem(z // (tile // (NY * block)) + k, tiles)
            rows = pl.ds(pl.multiple_of(t * tile, tile), tile)
            here = xs[rows, :]
            fresh = (
                COEF_A * here.astype(F32) + jnp.dot(here, poly[...], preferred_element_type=F32)
            ).astype(BF16)
            if not last_one:
                xs[rows, :] = fresh
                return carry
            final = factor * fresh.astype(F32)
            upd[rows, :] = final[:, :main].astype(BF16)
            ends = final[:, main:].reshape(tile // block, 2, block // 2, LANES)
            ends = ends[:, 0] + pltpu.roll(ends[:, 1], tail, 2)
            tails_out[pl.ds(t * (tile // block), tile // block)] = ends.astype(BF16)

            def one(j, inner):
                target = t * (tile // block) + j
                to_z, to_y = target // NY, target % NY
                send_to(
                    rows_at(upd, target * block, block),
                    out_ref.at[me, :, pl.ds(0, main)],
                    u_sem,
                    to_z,
                    to_y,
                )
                send_to(tails_out.at[target], tails_in.at[me], t_sem, to_z, to_y)
                return inner

            lax.fori_loop(0, tile // block, one, 0)
            return carry

        lax.fori_loop(0, padded // tile, make_gram, 0)
        lax.fori_loop(0, padded // tile, make_poly, 0)
        lax.fori_loop(0, tiles, make_iterate, 0)

    section_copy.wait_send()
    others = n_dp - 1
    take(mrecv.at[pl.ds(0, others * block)], m_sem.at[0])
    take(grecv.at[pl.ds(0, others * CAP)], g_sem.at[0])
    take(pmsend.at[pl.ds(0, (nz - 1) * PAD)], p_sem.at[0])
    take(frecv.at[pl.ds(0, nz * (NY - 1) * CAP)], y_sem.at[0])
    for part, way, sign, count in ways:
        for step in range(count):
            ring_copy(part, way, sign, step).wait_send()
    take(upd.at[pl.ds(0, others * block)], u_sem.at[0])
    take(tails_out.at[pl.ds(0, others)], t_sem.at[0])
    take(tails_in, t_sem.at[1])
    take(out_ref.at[:, :, pl.ds(0, main)], u_sem.at[1])
    ends = tails_in[...].astype(F32)
    ends = jnp.concatenate([ends, pltpu.roll(ends, tail, 2)], axis=1)
    out_ref[:, :, main:] = ends[:, :, :tail].astype(BF16)


def on_device(section_rows, embedded, norm_gain, routes, out_grad, momentum):
    n_dp = lax.axis_size("dp")
    n_sec = lax.axis_size("section")
    nz = n_dp // NY
    half = nz // 2
    tokens, top, hidden = out_grad.shape[1:]
    experts, block = momentum.shape[1:3]
    width = norm_gain.shape[1]
    padded = -(-hidden // 256) * 256
    main = hidden // LANES * LANES
    slots = n_dp * CAP
    vmem = pl.BlockSpec(memory_space=pltpu.VMEM)
    pair = pltpu.SemaphoreType.DMA((2,))
    return pl.pallas_call(
        functools.partial(kernel, n_dp, n_sec),
        out_shape=jax.ShapeDtypeStruct((experts, block, hidden), BF16),
        in_specs=[vmem] * 6,
        out_specs=vmem,
        scratch_shapes=[
            pltpu.VMEM(section_rows.shape[1:], BF16),
            pltpu.VMEM((nz * tokens, width), BF16),
            pltpu.VMEM((top, nz * PAD, tokens), BF16),
            pltpu.VMEM((nz * PAD, tokens), F32),
            pltpu.VMEM((nz * PAD, tokens), F32),
            pltpu.VMEM((top * tokens, padded), BF16),
            pltpu.VMEM((slots, padded), BF16),
            pltpu.VMEM((n_dp * block, main), BF16),
            pltpu.VMEM((slots, padded), BF16),
            pltpu.VMEM((slots, width), BF16),
            pltpu.VMEM((slots, width), BF16),
            pltpu.VMEM((width, padded), F32),
            pltpu.VMEM((width, padded), BF16),
            pltpu.VMEM((padded, padded), BF16),
            pltpu.VMEM((padded, padded), BF16),
            pltpu.VMEM((width, main), BF16),
            pltpu.VMEM((n_dp, block // 2, LANES), BF16),
            pltpu.VMEM((n_dp, block // 2, LANES), BF16),
            pair,
            pair,
            pair,
            pair,
            pair,
            pair,
            pair,
            pltpu.SemaphoreType.DMA((4, half)),
            pltpu.SemaphoreType.DMA((4, half)),
        ],
        compiler_params=pltpu.CompilerParams(
            collective_id=0, has_side_effects=True, vmem_limit_bytes=56 * 1024 * 1024
        ),
        name="muon_update",
    )(
        section_rows[0],
        embedded,
        norm_gain,
        jnp.transpose(routes, (2, 0, 1)),
        jnp.transpose(out_grad[0], (1, 2, 0)),
        momentum[0],
    )[None]


def solution(mesh):
    in_specs = (
        P("section", "dp", None),
        P("dp", None),
        P("section", None),
        P("section", "dp", None),
        P("section", "dp", None, None),
        P("section", None, "dp", None),
    )
    out_specs = P("section", None, "dp", None)
    return jax.shard_map(
        on_device, mesh=mesh, in_specs=in_specs, out_specs=out_specs, check_vma=False
    )
```

```python
import functools
import math

import jax
import jax.numpy as jnp
from jax import lax
from jax.experimental import pallas as pl
from jax.experimental.pallas import tpu as pltpu
from jax.sharding import PartitionSpec as P

MESH = pl.DeviceIdType.MESH
F32 = jnp.float32
BF16 = jnp.bfloat16

NS_ITERS = 2
COEF_A = 3.4445
COEF_B = -4.775
COEF_C = 2.0315
MOMENTUM_RATE = 0.95
NORM_EPS = 1e-06

NY = 4
CAP = 16
PAD = 8
LANES = 128

SCHEDULE = (32, 32, 40, 48, 56, 64, 68, 72, 76, 80, 128)


def iota(shape, dim):
    return lax.broadcasted_iota(jnp.int32, shape, dim)


def kernel(
    n_dp,
    n_sec,
    rows_ref,
    emb_ref,
    gain_ref,
    routes_ref,
    gt_ref,
    mom_ref,
    out_ref,
    rrecv,
    fall,
    wk,
    pmsend,
    pmrecv,
    gsc,
    gsend,
    mrecv,
    grecv,
    ysend,
    frecv,
    bl,
    xs,
    gram,
    poly,
    upd,
    tails_out,
    tails_in,
    x_sem,
    m_sem,
    g_sem,
    p_sem,
    y_sem,
    u_sem,
    t_sem,
    ring_send,
    ring_recv,
):
    nz = n_dp // NY
    half = nz // 2
    top, hidden, tokens = gt_ref.shape
    width = gain_ref.shape[1]
    block = mom_ref.shape[1]
    main = mrecv.shape[1]
    padded = grecv.shape[1]
    tail = hidden - main
    group = NY * CAP

    me = lax.axis_index("dp")
    sec = lax.axis_index("section")
    z = me // NY
    y = me % NY

    def wrap(index):
        return lax.rem(index + nz, nz)

    def remote(src, dst, sems, to_z, to_y):
        return pltpu.make_async_remote_copy(
            src_ref=src,
            dst_ref=dst,
            send_sem=sems.at[0],
            recv_sem=sems.at[1],
            device_id=(to_z * NY + to_y, sec),
            device_id_type=MESH,
        )

    def take(ref, sem):
        pltpu.make_async_copy(ref, ref, sem).wait()

    def rows_at(ref, start, size):
        return ref.at[pl.ds(pl.multiple_of(start, size), size)]

    barrier = pltpu.get_barrier_semaphore()
    after = lax.rem(sec + 1, n_sec)
    before = lax.rem(sec + n_sec - 1, n_sec)

    def greet(k, carry):
        step = (k + 1) // 2
        to = me + n_dp // 2 + jnp.where(k % 2 == 1, step, n_dp - step)
        pl.semaphore_signal(
            barrier, inc=1, device_id=(lax.rem(to, n_dp), sec), device_id_type=MESH
        )
        return carry

    lax.fori_loop(0, n_dp - 1, greet, 0)
    for other in (after, before):
        pl.semaphore_signal(barrier, inc=1, device_id=(me, other), device_id_type=MESH)
    pl.semaphore_wait(barrier, n_dp + 1)

    section_copy = pltpu.make_async_remote_copy(
        src_ref=rows_ref,
        dst_ref=rrecv,
        send_sem=x_sem.at[0],
        recv_sem=x_sem.at[1],
        device_id=(me, after),
        device_id_type=MESH,
    )
    section_copy.start()

    same_parity = lax.rem(z, 2)

    def offset(phase, jz):
        near = half - 2 * ((jz + 1) // 2)
        near = jnp.where(jz % 2 == 1, near, -near)
        odd = half - 1 - 2 * (jz // 2)
        odd = jnp.where(jz % 2 == 0, odd, -odd)
        return jnp.where(same_parity == phase, near, odd)

    def send_to(src, dst, sems, to_z, to_y):
        target = to_z * NY + to_y

        @pl.when(target != me)
        def _():
            remote(src, dst, sems, to_z, to_y).start()

        @pl.when(target == me)
        def _():
            pltpu.make_async_copy(src, dst, sems.at[1]).start()

    share = half * NY

    def stream(lo, hi):
        for part in range(4):
            first, last = max(lo, part * share), min(hi, (part + 1) * share)
            if first < last:
                lax.fori_loop(
                    first - part * share,
                    last - part * share,
                    functools.partial(send_block, part // 2, part % 2 == 1),
                    0,
                )

    def send_block(phase, cotangents, j, carry):
        to_z = wrap(z + offset(phase, j // NY))
        if cotangents:
            to_y = j % NY
            src = rows_at(gsend, (phase * share + j) * CAP, CAP)
            send_to(src, rows_at(grecv, CAP * me, CAP), g_sem, to_z, to_y)
        else:
            to_y = lax.rem(y + j, NY)
            src = mom_ref.at[to_z * NY + to_y, :, pl.ds(0, main)]
            send_to(src, rows_at(mrecv, block * me, block), m_sem, to_z, to_y)
        return carry

    stream(0, SCHEDULE[0])

    table = nz * PAD
    expert = iota((table, tokens), 0)
    expert = jnp.where(expert % PAD < NY, (expert // PAD) * NY + expert % PAD, -1)
    named = jnp.zeros((table, tokens), F32)
    for k in range(top):
        named += jnp.where(routes_ref[k] == expert, 1.0, 0.0)
    earlier = jnp.where(iota((tokens, tokens), 0) < iota((tokens, tokens), 1), 1.0, 0.0)
    place = jnp.dot(named.astype(BF16), earlier.astype(BF16), preferred_element_type=F32)
    for k in range(top):
        wk[k] = jnp.where(routes_ref[k] == expert, place, -1.0).astype(BF16)
    pmsend[...] = jnp.where(named > 0.0, place, -1.0)

    def send_places(dz, carry):
        to_z = wrap(z + dz)
        send_to(rows_at(pmsend, PAD * to_z, PAD), rows_at(pmrecv, PAD * z, PAD), p_sem, to_z, y)
        return carry

    lax.fori_loop(0, nz, send_places, 0)

    for k in range(top):
        widened = jnp.concatenate(
            [gt_ref[k], jnp.zeros((padded - hidden, tokens), BF16)], axis=0
        )
        gsc[k * tokens : (k + 1) * tokens, :] = widened.T

    slots = 4 * group
    shift = jnp.where(
        iota((tail, LANES), 1) == iota((tail, LANES), 0) + (LANES - tail), 1.0, 0.0
    ).astype(BF16)
    chunks = half // 4

    def pack(phase, q):
        base = (phase * chunks + q) * slots
        to = [wrap(z + offset(phase, 4 * q + i)) for i in range(4)]
        which = iota((slots, table), 0)
        row = jnp.zeros((slots, table), jnp.int32)
        for i in range(4):
            row = jnp.where(which // group == i, to[i] * PAD, row)
        row = row + (which // CAP) % NY
        spread = jnp.where(iota((slots, table), 1) == row, 1.0, 0.0).astype(BF16)
        spot = (iota((slots, tokens), 0) % CAP).astype(F32)
        picks = []
        for k in range(top):
            at = jnp.dot(spread, wk[k], preferred_element_type=F32)
            picks.append(jnp.where(at == spot, 1.0, 0.0).astype(BF16))
        chosen = jnp.dot(jnp.concatenate(picks, axis=1), gsc[...], preferred_element_type=F32)
        gsend[base : base + slots, :main] = chosen[:, :main].astype(BF16)
        tails = jnp.concatenate(
            [
                mom_ref[pl.ds(to[i] * NY, NY), :, main:hidden].reshape(NY * block, tail)
                for i in range(4)
            ],
            axis=0,
        )
        gsend[base : base + slots, main:] = (
            chosen[:, main:] + jnp.dot(tails, shift, preferred_element_type=F32)
        ).astype(BF16)

    for phase in range(2):
        for q in range(chunks):
            pack(phase, q)
    stream(SCHEDULE[0], SCHEDULE[1])

    section_copy.wait_recv()
    values = jnp.where(sec == 0, emb_ref[...], rrecv[...]).astype(F32)
    inverse = lax.rsqrt(jnp.mean(values * values, axis=-1, keepdims=True) + NORM_EPS)
    fall[pl.ds(pl.multiple_of(z * tokens, tokens), tokens), :] = (
        values[:, :width] * inverse * gain_ref[...]
    ).astype(BF16)

    parts = 2
    piece = tokens // parts
    ways = tuple(
        (part, way, sign, half - (part + way) % 2)
        for part in range(parts)
        for way, sign in ((0, 1), (1, -1))
    )

    def ring_copy(part, way, sign, step):
        held = rows_at(fall, wrap(z - sign * step) * tokens + part * piece, piece)
        return pltpu.make_async_remote_copy(
            src_ref=held,
            dst_ref=held,
            send_sem=ring_send.at[2 * part + way, step],
            recv_sem=ring_recv.at[2 * part + way, step],
            device_id=(wrap(z + sign) * NY + y, sec),
            device_id_type=MESH,
        )

    def ring_step(step):
        for part, way, sign, count in ways:
            if 1 <= step <= count:
                ring_copy(part, way, sign, step - 1).wait_recv()
            if step < count:
                ring_copy(part, way, sign, step).start()

    def pick(source):
        places = pmrecv[pl.ds(pl.multiple_of(source * PAD, PAD), PAD), :]
        at = jnp.concatenate(
            [jnp.broadcast_to(places[i : i + 1, :], (CAP, tokens)) for i in range(NY)], axis=0
        )
        spot = (iota((group, tokens), 0) % CAP).astype(F32)
        chosen = jnp.dot(
            jnp.where(at == spot, 1.0, 0.0).astype(BF16),
            fall[pl.ds(pl.multiple_of(source * tokens, tokens), tokens), :],
            preferred_element_type=F32,
        )
        ysend[pl.ds(pl.multiple_of(source * group, group), group), :] = chosen.astype(BF16)
        for dy in range(NY):
            to_y = lax.rem(y + dy, NY)
            src = rows_at(ysend, source * group + to_y * CAP, CAP)
            dst = rows_at(frecv, (source * NY + y) * CAP, CAP)
            if dy == 0:
                pltpu.make_async_copy(src, dst, y_sem.at[1]).start()
            else:
                remote(src, dst, y_sem, z, to_y).start()

    def pick_step(step):
        pick(wrap(z + step))
        if 0 < step < half:
            pick(wrap(z - step))

    for step in range(half + 1):
        ring_step(step)
        if step == 0:
            take(pmrecv, p_sem.at[1])
        pick_step(step)
        stream(SCHEDULE[step + 1], SCHEDULE[step + 2])

    take(frecv, y_sem.at[1])
    take(grecv, g_sem.at[1])
    take(mrecv, m_sem.at[1])
    tile = 256
    tiles = width // tile

    def blend(t, total):
        rows = pl.ds(pl.multiple_of(t * tile, tile), tile)
        cols = pl.ds(pl.multiple_of(t * tile, tile), tile)
        gradient = lax.dot_general(
            frecv[:, cols], grecv[...], (((0,), (0,)), ((), ())), preferred_element_type=F32
        )

        def mixed(grad, mom):
            return grad + MOMENTUM_RATE * (MOMENTUM_RATE * mom + grad)

        first = mixed(gradient[:, :main], mrecv[rows, :].astype(F32))
        rest = pltpu.roll(grecv[rows, main:].astype(F32), tail, 1)
        last = mixed(gradient[:, main:], rest)
        last = jnp.where(iota(last.shape, 1) < tail, last, 0.0)
        bl[rows, :main] = first
        bl[rows, main:] = last
        return total + jnp.sum(first * first) + jnp.sum(last * last)

    total = lax.fori_loop(0, tiles, blend, jnp.zeros((), F32))
    scale = 1.0 / (jnp.sqrt(jnp.full((1, 1), total, F32)) + 1e-07)

    def normalize(t, carry):
        rows = pl.ds(pl.multiple_of(t * tile, tile), tile)
        xs[rows, :] = (bl[rows, :] * scale).astype(BF16)
        return carry

    lax.fori_loop(0, tiles, normalize, 0)

    factor = 0.2 * math.sqrt(width)
    for repeat in range(NS_ITERS):
        last_one = repeat == NS_ITERS - 1

        def make_gram(t, carry):
            cols = pl.ds(pl.multiple_of(t * tile, tile), tile)
            gram[cols, :] = lax.dot_general(
                xs[:, cols], xs[...], (((0,), (0,)), ((), ())), preferred_element_type=F32
            ).astype(BF16)
            return carry

        def make_poly(t, carry):
            rows = pl.ds(pl.multiple_of(t * tile, tile), tile)
            here = gram[rows, :]
            squared = jnp.dot(here, gram[...], preferred_element_type=F32)
            poly[rows, :] = (COEF_B * here.astype(F32) + COEF_C * squared).astype(BF16)
            return carry

        def make_iterate(k, carry):
            t = lax.rem(z // (tile // (NY * block)) + k, tiles)
            rows = pl.ds(pl.multiple_of(t * tile, tile), tile)
            here = xs[rows, :]
            fresh = (
                COEF_A * here.astype(F32) + jnp.dot(here, poly[...], preferred_element_type=F32)
            ).astype(BF16)
            if not last_one:
                xs[rows, :] = fresh
                return carry
            final = factor * fresh.astype(F32)
            upd[rows, :] = final[:, :main].astype(BF16)
            ends = final[:, main:].reshape(tile // block, 2, block // 2, LANES)
            ends = ends[:, 0] + pltpu.roll(ends[:, 1], tail, 2)
            tails_out[pl.ds(t * (tile // block), tile // block)] = ends.astype(BF16)

            def one(j, inner):
                target = t * (tile // block) + j
                to_z, to_y = target // NY, target % NY
                send_to(
                    rows_at(upd, target * block, block),
                    out_ref.at[me, :, pl.ds(0, main)],
                    u_sem,
                    to_z,
                    to_y,
                )
                send_to(tails_out.at[target], tails_in.at[me], t_sem, to_z, to_y)
                return inner

            lax.fori_loop(0, tile // block, one, 0)
            return carry

        lax.fori_loop(0, padded // tile, make_gram, 0)
        lax.fori_loop(0, padded // tile, make_poly, 0)
        lax.fori_loop(0, tiles, make_iterate, 0)

    section_copy.wait_send()
    others = n_dp - 1
    take(mrecv.at[pl.ds(0, others * block)], m_sem.at[0])
    take(grecv.at[pl.ds(0, others * CAP)], g_sem.at[0])
    take(pmsend.at[pl.ds(0, (nz - 1) * PAD)], p_sem.at[0])
    take(frecv.at[pl.ds(0, nz * (NY - 1) * CAP)], y_sem.at[0])
    for part, way, sign, count in ways:
        for step in range(count):
            ring_copy(part, way, sign, step).wait_send()
    take(upd.at[pl.ds(0, others * block)], u_sem.at[0])
    take(tails_out.at[pl.ds(0, others)], t_sem.at[0])
    take(tails_in, t_sem.at[1])
    take(out_ref.at[:, :, pl.ds(0, main)], u_sem.at[1])
    ends = tails_in[...].astype(F32)
    ends = jnp.concatenate([ends, pltpu.roll(ends, tail, 2)], axis=1)
    out_ref[:, :, main:] = ends[:, :, :tail].astype(BF16)


def on_device(section_rows, embedded, norm_gain, routes, out_grad, momentum):
    n_dp = lax.axis_size("dp")
    n_sec = lax.axis_size("section")
    nz = n_dp // NY
    half = nz // 2
    tokens, top, hidden = out_grad.shape[1:]
    experts, block = momentum.shape[1:3]
    width = norm_gain.shape[1]
    padded = -(-hidden // 256) * 256
    main = hidden // LANES * LANES
    slots = n_dp * CAP
    vmem = pl.BlockSpec(memory_space=pltpu.VMEM)
    pair = pltpu.SemaphoreType.DMA((2,))
    return pl.pallas_call(
        functools.partial(kernel, n_dp, n_sec),
        out_shape=jax.ShapeDtypeStruct((experts, block, hidden), BF16),
        in_specs=[vmem] * 6,
        out_specs=vmem,
        scratch_shapes=[
            pltpu.VMEM(section_rows.shape[1:], BF16),
            pltpu.VMEM((nz * tokens, width), BF16),
            pltpu.VMEM((top, nz * PAD, tokens), BF16),
            pltpu.VMEM((nz * PAD, tokens), F32),
            pltpu.VMEM((nz * PAD, tokens), F32),
            pltpu.VMEM((top * tokens, padded), BF16),
            pltpu.VMEM((slots, padded), BF16),
            pltpu.VMEM((n_dp * block, main), BF16),
            pltpu.VMEM((slots, padded), BF16),
            pltpu.VMEM((slots, width), BF16),
            pltpu.VMEM((slots, width), BF16),
            pltpu.VMEM((width, padded), F32),
            pltpu.VMEM((width, padded), BF16),
            pltpu.VMEM((padded, padded), BF16),
            pltpu.VMEM((padded, padded), BF16),
            pltpu.VMEM((width, main), BF16),
            pltpu.VMEM((n_dp, block // 2, LANES), BF16),
            pltpu.VMEM((n_dp, block // 2, LANES), BF16),
            pair,
            pair,
            pair,
            pair,
            pair,
            pair,
            pair,
            pltpu.SemaphoreType.DMA((4, half)),
            pltpu.SemaphoreType.DMA((4, half)),
        ],
        compiler_params=pltpu.CompilerParams(
            collective_id=0, has_side_effects=True, vmem_limit_bytes=56 * 1024 * 1024
        ),
        name="muon_update",
    )(
        section_rows[0],
        embedded,
        norm_gain,
        jnp.transpose(routes, (2, 0, 1)),
        jnp.transpose(out_grad[0], (1, 2, 0)),
        momentum[0],
    )[None]


def solution(mesh):
    in_specs = (
        P("section", "dp", None),
        P("dp", None),
        P("section", None),
        P("section", "dp", None),
        P("section", "dp", None, None),
        P("section", None, "dp", None),
    )
    out_specs = P("section", None, "dp", None)
    return jax.shard_map(
        on_device, mesh=mesh, in_specs=in_specs, out_specs=out_specs, check_vma=False
    )
```
